768 devices in a mesh: dp: 96 (over z_lo, y, core), mp: 8 (over z_hi, x).
Axes of the slice: x: 4, y: 8, z: 12 (z_hi: 2, z_lo: 6; z = z_hi * 6 + z_lo), core: 2. Of those that a mesh axis runs over, the one named last changes fastest.
Arguments:
- patches: bfloat16 [192, 1024, 1152], P('dp'), may hold values from -6 to 6
- counts: int32 [192], P('dp'), may hold values from 256 to 1024, as said below
- pos_text: int32 [192], P('dp'), may hold values from 0 to 191, each once
- texts: bfloat16 [192, 1152], P('dp'), may hold values from -6 to 6
- kv_weight: bfloat16 [1152, 2, 1152], P(None, None, 'mp'), may hold values from -0.1875 to 0.1875
- out_weight: bfloat16 [1152, 1152], P('mp'), may hold values from -0.1875 to 0.1875
- query: float32 [1152], P('mp')
- logit_scale: float32 [1], replicated, may hold values from 4 to 16
- logit_bias: float32 [1], replicated, may hold values from -4 to -2
Outputs:
- kv_grad: float32 [1152, 2, 1152], P('dp', None, 'mp')
- out_grad: float32 [1152, 1152], P('mp', 'dp')
- text_grad: float32 [192, 1152], P('dp')
The draws below stay inside these ranges and needn't reach their ends.
Inputs may be any that keep to these rules, and one draw needn't show every extreme that they name: `counts`: some image has exactly 1024 live patches and some exactly 256. `pos_text`: each text is paired with exactly one image.
All inputs are finite; a program needn't handle non-finite values.
Results may differ from the reference program's by a relative error of at most 0.0085.
The reference program's roundings to bfloat16 on the way count: a program that leaves them out, or rounds other values in their place, can miss the bound.
Values may be sent and summed in bfloat16 or wider, within the bound.
No kernel may reach another device: no remote copies, remote signals or barrier semaphores. Data moves between devices by JAX's collectives and lax.ppermute only.
A program may use at most 64 MiB of HBM per device.

```python
import math
import jax
import jax.numpy as jnp
from jax import lax

HEADS = 16
HEAD_DIM = 72
D = 1152
MAXP = 1024
IMAGES = 192
TEXTS = 192


def draw_counts(key, part):
    key = jax.random.fold_in(key, 11)
    first_key, second_key = jax.random.split(key)
    drawn = jax.random.randint(first_key, (IMAGES,), MAXP // 4, MAXP + 1)
    spots = jax.random.permutation(second_key, IMAGES)
    drawn = drawn.at[spots[0]].set(MAXP)
    drawn = drawn.at[spots[1]].set(MAXP // 4)
    return drawn.astype(jnp.int32)


def draw_query(key, part):
    key = jax.random.fold_in(key, 23)
    first_key, second_key = jax.random.split(key)
    lowest = math.log(0.5)
    highest = math.log(4.0)
    head_scales = jnp.exp(jax.random.uniform(first_key, (HEADS,), jnp.float32, lowest, highest))
    values = jax.random.normal(second_key, (HEADS, HEAD_DIM), jnp.float32) * head_scales[:, None]
    return values.reshape(HEADS * HEAD_DIM).astype(jnp.float32)


def steps_of(key, dims, cuts, least, high):
    def one(position, shards_of):
        draws = jax.random.uniform(jax.random.fold_in(jax.random.fold_in(key, 6), position), (shards_of,), jnp.float32, least / len(cuts), high / len(cuts))
        return jnp.repeat(jnp.exp(draws), dims[position] // shards_of).reshape((-1,) + (1,) * (len(dims) - position - 1))

    level = one(*cuts[0])
    for cut in cuts[1:]:
        level = level * one(*cut)
    return level


def bell_draw(stream_key, extent, width, most, shards=(), kind=jnp.bfloat16):
    values = width * jax.random.normal(stream_key, extent, jnp.float32)
    if shards:
        values = values * steps_of(stream_key, extent, shards, -0.22, 0.18)
    return jnp.clip(values, -most, most).astype(kind)


def setup_inputs(seed: int = 0) -> dict:
    key_list = jax.random.split(jax.random.key(seed), 10)
    patches = bell_draw(key_list[0], (IMAGES, MAXP, D), 1.0, 6.0, ((0, 96),))
    counts = draw_counts(jax.random.fold_in(key_list[9], 71), 0)
    pos_text = jax.random.permutation(key_list[2], IMAGES).astype(jnp.int32)
    texts = bell_draw(key_list[3], (TEXTS, D), 1.0, 6.0, ((0, 96),))
    kv_weight = bell_draw(key_list[4], (D, 2, D), D ** -0.5, 0.1875, ((2, 8),))
    out_weight = bell_draw(key_list[5], (D, D), D ** -0.5, 0.1875, ((0, 8),))
    query = draw_query(jax.random.fold_in(key_list[9], 71), 0)
    logit_scale = jnp.clip(jnp.exp(jax.random.uniform(key_list[7], (1,), jnp.float32, math.log(4.0), math.log(16.0))), 4.0, 16.0)
    logit_bias = jnp.clip(jax.random.uniform(key_list[8], (1,), jnp.float32, -4.0, -2.0), -4.0, -2.0)
    return {"patches": patches, "counts": counts, "pos_text": pos_text, "texts": texts, "kv_weight": kv_weight, "out_weight": out_weight, "query": query, "logit_scale": logit_scale, "logit_bias": logit_bias}


def unit_rows(values):
    row_norms = jnp.sqrt(lax.optimization_barrier(jnp.sum(values * values, axis=1, keepdims=True)) + 1e-06)
    return (values / row_norms, row_norms)

def reference(patches, counts, pos_text, texts, kv_weight, out_weight, query, logit_scale, logit_bias):
    highest = lax.Precision.HIGHEST
    head_root = math.sqrt(HEAD_DIM)
    model_width = HEADS * HEAD_DIM
    w_key = kv_weight[:, 0, :].astype(jnp.float32).reshape(model_width, HEADS, HEAD_DIM)
    w_value = kv_weight[:, 1, :].astype(jnp.float32).reshape(model_width, HEADS, HEAD_DIM)
    q_heads = query.reshape(HEADS, HEAD_DIM)
    probe_vec = (jnp.einsum('dhe,he->dh', w_key, q_heads, precision=highest) / head_root).astype(jnp.bfloat16)
    slot_index = jnp.arange(MAXP, dtype=jnp.int32)

    def forward_one(item):
        image_rows, live_count = item
        live_mask = (slot_index < live_count)[None, :]
        scores = jnp.dot(probe_vec.T, image_rows.T, preferred_element_type=jnp.float32)
        scores = jnp.where(live_mask, scores, -1e+30)
        peak = lax.optimization_barrier(jnp.max(scores, axis=1, keepdims=True))
        raised = jnp.where(live_mask, jnp.exp(scores - peak), 0.0)
        attend = raised / lax.optimization_barrier(jnp.sum(raised, axis=1, keepdims=True))
        moments = jnp.dot(attend.astype(jnp.bfloat16), image_rows, preferred_element_type=jnp.float32)
        return (attend, moments.astype(jnp.bfloat16))
    attend, moments16 = lax.map(forward_one, (patches, counts))
    moments_f = moments16.astype(jnp.float32)
    pooled = jnp.einsum('bhd,dhe->bhe', moments_f, w_value, precision=highest).reshape(IMAGES, model_width)
    pooled16 = pooled.astype(jnp.bfloat16)
    embedding = jnp.dot(pooled16, out_weight, preferred_element_type=jnp.float32)
    image_unit, image_norm = unit_rows(embedding)
    text_unit, text_norm = unit_rows(texts.astype(jnp.float32))
    temper = logit_scale[0]
    offset = logit_bias[0]
    logits = temper * jnp.dot(image_unit, text_unit.T, precision=highest) + offset
    pair_sign = jnp.where(pos_text[:, None] == jnp.arange(TEXTS, dtype=jnp.int32)[None, :], 1.0, -1.0)
    slopes = -pair_sign * jax.nn.sigmoid(-pair_sign * logits)
    grad_img = temper * jnp.dot(slopes, text_unit, precision=highest)
    grad_txt = temper * jnp.dot(slopes.T, image_unit, precision=highest)
    text_grad = (grad_txt - text_unit * lax.optimization_barrier(jnp.sum(text_unit * grad_txt, axis=1, keepdims=True))) / text_norm
    grad_embed = (grad_img - image_unit * lax.optimization_barrier(jnp.sum(image_unit * grad_img, axis=1, keepdims=True))) / image_norm
    grad_pooled = jnp.dot(grad_embed, out_weight.astype(jnp.float32).T, precision=highest)
    grad_heads = grad_pooled.reshape(IMAGES, HEADS, HEAD_DIM)
    grad_moments = jnp.einsum('bhe,dhe->bhd', grad_heads, w_value, precision=highest).astype(jnp.bfloat16)

    def backward_one(item):
        image_rows, attend_one, grad_one = item
        grad_attend = jnp.dot(grad_one, image_rows.T, preferred_element_type=jnp.float32)
        grad_scores = attend_one * (grad_attend - lax.optimization_barrier(jnp.sum(attend_one * grad_attend, axis=1, keepdims=True)))
        return jnp.dot(grad_scores.astype(jnp.bfloat16), image_rows, preferred_element_type=jnp.float32)
    key_moments = lax.map(backward_one, (patches, attend, grad_moments))
    key_grad = (jnp.einsum('bhd,he->dhe', key_moments, q_heads, precision=highest) / head_root).reshape(model_width, model_width)
    value_grad = jnp.einsum('bhd,bhe->dhe', moments_f, grad_heads, precision=highest).reshape(model_width, model_width)
    kv_grad = jnp.stack([key_grad, value_grad], axis=1)
    out_grad = jnp.dot(pooled16.astype(jnp.float32).T, grad_embed, precision=highest)
    return (kv_grad, out_grad, text_grad)
```

```python
import math

import jax
import jax.numpy as jnp
from jax import lax
from jax.sharding import PartitionSpec as P

HEAD_DIM = 72
ZL, YC = 6, 16
ZL_GROUPS = [[z * YC + r for z in range(ZL)] for r in range(YC)]
YC_GROUPS = [[z * YC + r for r in range(YC)] for z in range(ZL)]
HIGHEST = lax.Precision.HIGHEST


def spread(block, groups):
    n = len(groups[0])
    copies = jnp.broadcast_to(block[None], (n,) + block.shape)
    return lax.all_to_all(copies, "dp", 0, 0, axis_index_groups=groups, tiled=True)


def split2(values):
    high = values.astype(jnp.bfloat16)
    low = (values - high.astype(jnp.float32)).astype(jnp.bfloat16)
    return high, low


def local(patches, counts, pos_text, texts, kv_weight, out_weight, query, logit_scale, logit_bias):
    head_root = math.sqrt(HEAD_DIM)
    images, slot_count, width = patches.shape
    local_width = kv_weight.shape[2]
    heads = local_width // HEAD_DIM
    dp = ZL * YC
    total = dp * images
    rows = width // dp
    me = lax.axis_index("dp")
    temper = logit_scale[0]
    offset = logit_bias[0]

    label = jnp.broadcast_to(pos_text.astype(jnp.bfloat16)[:, None], (images, 128))
    text_block = jnp.concatenate([texts, label], axis=1)
    text_zl = spread(text_block, ZL_GROUPS)
    text_all = spread(text_zl, YC_GROUPS)

    q_heads = query.reshape(heads, HEAD_DIM)
    w_key = kv_weight[:, 0, :].astype(jnp.float32).reshape(width, heads, HEAD_DIM)
    w_value = kv_weight[:, 1, :].reshape(width, heads, HEAD_DIM)
    probe = (jnp.einsum("dhe,he->dh", w_key, q_heads, precision=HIGHEST) / head_root).astype(
        jnp.bfloat16
    )
    live = (jnp.arange(slot_count, dtype=jnp.int32)[None, :] < counts[:, None])[:, None, :]
    scores = jnp.einsum("bpd,dh->bhp", patches, probe, preferred_element_type=jnp.float32)
    scores = jnp.where(live, scores, -1e30)
    peak = jnp.max(scores, axis=2, keepdims=True)
    raised = jnp.where(live, jnp.exp(scores - peak), 0.0)
    attend = raised / jnp.sum(raised, axis=2, keepdims=True)
    moments16 = jnp.einsum(
        "bhp,bpd->bhd", attend.astype(jnp.bfloat16), patches, preferred_element_type=jnp.float32
    ).astype(jnp.bfloat16)
    pooled16 = (
        jnp.einsum("bhd,dhe->bhe", moments16, w_value, preferred_element_type=jnp.float32)
        .reshape(images, local_width)
        .astype(jnp.bfloat16)
    )
    partial_value = jnp.dot(pooled16, out_weight, preferred_element_type=jnp.float32)

    mp = lax.axis_size("mp")
    parts = lax.all_to_all(
        jnp.broadcast_to(partial_value[None], (mp, images, width)), "mp", 0, 0, tiled=True
    )
    embedding = jnp.sum(parts, axis=0)

    image_block = jnp.concatenate([embedding, pooled16.astype(jnp.float32)], axis=1)
    image_zl = spread(image_block, ZL_GROUPS)

    text_rows = text_all.reshape(total, width + 128)
    text16 = text_rows[:, :width]
    labels = text_rows[:, width].astype(jnp.int32)
    place = jnp.arange(total, dtype=jnp.int32)
    ids = ((place // images % ZL) * YC + place // (images * ZL)) * images + place % images
    text_f = text16.astype(jnp.float32)
    text_norm = jnp.sqrt(jnp.sum(text_f * text_f, axis=1) + 1e-06)
    text_unit = text_f / text_norm[:, None]

    def pairs(emb, pos):
        norm = jnp.sqrt(jnp.sum(emb * emb, axis=1, keepdims=True) + 1e-06)
        unit = emb / norm
        cosine = jnp.dot(unit, text_unit.T, precision=HIGHEST)
        sign = jnp.where(pos[:, None] == ids[None, :], 1.0, -1.0)
        slope = -sign * jax.nn.sigmoid(-sign * (temper * cosine + offset))
        grad = temper * jnp.dot(slope, text_unit, precision=HIGHEST)
        grad = (grad - unit * jnp.sum(unit * grad, axis=1, keepdims=True)) / norm
        pooled_grad = jnp.dot(grad, out_weight.astype(jnp.float32).T, precision=HIGHEST)
        return unit, slope, grad, pooled_grad

    grad_heads = pairs(embedding, pos_text)[3].reshape(images, heads, HEAD_DIM)
    grad_moments = jnp.einsum(
        "bhe,dhe->bhd", grad_heads, w_value.astype(jnp.float32), precision=HIGHEST
    ).astype(jnp.bfloat16)
    image_all = spread(image_zl, YC_GROUPS)
    grad_attend = jnp.einsum(
        "bpd,bhd->bhp", patches, grad_moments, preferred_element_type=jnp.float32
    )
    grad_scores = attend * (grad_attend - jnp.sum(attend * grad_attend, axis=2, keepdims=True))
    key_moments = jnp.einsum(
        "bhp,bpd->hd",
        grad_scores.astype(jnp.bfloat16),
        patches,
        preferred_element_type=jnp.float32,
    )

    rows_block = jnp.concatenate(
        [key_moments, moments16.astype(jnp.float32).reshape(images * heads, width)], axis=0
    )
    count = heads + images * heads
    sent = rows_block.reshape(count, dp, rows).transpose(1, 0, 2).reshape(dp, count * rows)
    sent = jnp.pad(sent, ((0, 0), (0, 128 - count * rows)))
    got = lax.all_to_all(sent, "dp", 0, 0, tiled=True)

    image_rows = image_all.reshape(total, width + local_width)
    emb_all = image_rows[:, :width]
    pooled_all = image_rows[:, width:]
    unit_all, slope_all, grad_all, pooled_grad_all = pairs(emb_all, labels)
    mine = (ids[None, :] == me * images + jnp.arange(images, dtype=jnp.int32)[:, None]).astype(
        jnp.float32
    )
    own_slope = jnp.dot(mine, slope_all.T, precision=HIGHEST)
    grad_txt = temper * jnp.dot(own_slope, unit_all, precision=HIGHEST)
    own_text = texts.astype(jnp.float32)
    own_norm = jnp.sqrt(jnp.sum(own_text * own_text, axis=1, keepdims=True) + 1e-06)
    own_unit = own_text / own_norm
    text_grad = (
        grad_txt - own_unit * jnp.sum(own_unit * grad_txt, axis=1, keepdims=True)
    ) / own_norm
    own_columns = lax.dynamic_slice_in_dim(grad_all, me * rows, rows, axis=1)
    out_grad = jnp.dot(pooled_all.T, own_columns, precision=HIGHEST)

    got = got[:, : count * rows].reshape(ZL, YC, count, rows)
    key_sum = jnp.sum(got[:, :, :heads], axis=(0, 1))
    moments_all = (
        got[:, :, heads:]
        .reshape(ZL, YC, images, heads, rows)
        .transpose(1, 0, 2, 3, 4)
        .reshape(total, heads, rows)
    )
    key_grad = (key_sum.T[:, :, None] * q_heads[None] / head_root).reshape(rows, local_width)
    value_grad = jnp.einsum(
        "bhd,bhe->dhe",
        moments_all,
        pooled_grad_all.reshape(total, heads, HEAD_DIM),
        precision=HIGHEST,
    ).reshape(rows, local_width)
    kv_grad = jnp.stack([key_grad, value_grad], axis=1)
    return (kv_grad, out_grad, text_grad)


def solution(mesh):
    in_specs = (
        P("dp", None, None),
        P("dp"),
        P("dp"),
        P("dp", None),
        P(None, None, "mp"),
        P("mp", None),
        P("mp"),
        P(),
        P(),
    )
    out_specs = (P("dp", None, "mp"), P("mp", "dp"), P("dp", None))
    return jax.shard_map(local, mesh=mesh, in_specs=in_specs, out_specs=out_specs, check_vma=False)
```

```python
import math

import jax
import jax.numpy as jnp
from jax import lax
from jax.sharding import PartitionSpec as P

HEAD_DIM = 72
ZL, YC = 6, 16
ZL_GROUPS = [[z * YC + r for z in range(ZL)] for r in range(YC)]
YC_GROUPS = [[z * YC + r for r in range(YC)] for z in range(ZL)]
XS = 4
X_GROUPS = [list(range(XS)), list(range(XS, 2 * XS))]
HIGHEST = lax.Precision.HIGHEST


def spread(block, groups, axis):
    n = len(groups[0])
    copies = jnp.broadcast_to(block[None], (n,) + block.shape)
    return lax.all_to_all(copies, axis, 0, 0, axis_index_groups=groups, tiled=True)


def local(patches, counts, pos_text, texts, kv_weight, out_weight, query, logit_scale, logit_bias):
    head_root = math.sqrt(HEAD_DIM)
    images, slot_count, width = patches.shape
    local_width = kv_weight.shape[2]
    heads = local_width // HEAD_DIM
    dp = ZL * YC
    total = dp * images
    rows = width // dp
    temper = logit_scale[0]
    offset = logit_bias[0]

    text_zl = spread(texts, ZL_GROUPS, "dp")
    q_heads = query.reshape(heads, HEAD_DIM)
    w_key = kv_weight[:, 0, :].astype(jnp.float32).reshape(width, heads, HEAD_DIM)
    w_value = kv_weight[:, 1, :].reshape(width, heads, HEAD_DIM)
    probe = (jnp.einsum("dhe,he->dh", w_key, q_heads, precision=HIGHEST) / head_root).astype(
        jnp.bfloat16
    )
    live = (jnp.arange(slot_count, dtype=jnp.int32)[None, :] < counts[:, None])[:, None, :]
    scores = jnp.einsum("bpd,dh->bhp", patches, probe, preferred_element_type=jnp.float32)
    scores = jnp.where(live, scores, -1e30)
    peak = jnp.max(scores, axis=2, keepdims=True)
    raised = jnp.where(live, jnp.exp(scores - peak), 0.0)
    attend = raised / jnp.sum(raised, axis=2, keepdims=True)
    text_zl, attend = lax.optimization_barrier((text_zl, attend))
    text_all = spread(text_zl, YC_GROUPS, "dp")
    moments16 = jnp.einsum(
        "bhp,bpd->bhd", attend.astype(jnp.bfloat16), patches, preferred_element_type=jnp.float32
    ).astype(jnp.bfloat16)
    pooled16 = (
        jnp.einsum("bhd,dhe->bhe", moments16, w_value, preferred_element_type=jnp.float32)
        .reshape(images, local_width)
        .astype(jnp.bfloat16)
    )
    partial_value = jnp.dot(pooled16, out_weight, preferred_element_type=jnp.float32)

    along_x = lax.psum(partial_value, "mp", axis_index_groups=X_GROUPS)
    along_x, text_all = lax.optimization_barrier((along_x, text_all))
    mp = lax.axis_size("mp")
    embedding = along_x + lax.ppermute(
        along_x, "mp", [(i, (i + mp // 2) % mp) for i in range(mp)]
    )

    text_rows = text_all.transpose(1, 0, 2, 3).reshape(total, width)
    text_f = text_rows.astype(jnp.float32)
    text_norm = jnp.sqrt(jnp.sum(text_f * text_f, axis=1) + 1e-06)
    text_unit = text_f / text_norm[:, None]

    norm = jnp.sqrt(jnp.sum(embedding * embedding, axis=1, keepdims=True) + 1e-06)
    unit = embedding / norm
    cosine = jnp.dot(unit, text_unit.T, precision=HIGHEST)
    columns = jnp.arange(total, dtype=jnp.int32)
    sign = jnp.where(pos_text[:, None] == columns[None, :], 1.0, -1.0)
    slope = -sign * jax.nn.sigmoid(-sign * (temper * cosine + offset))
    grad = temper * jnp.dot(slope, text_unit, precision=HIGHEST)
    grad_embed = (grad - unit * jnp.sum(unit * grad, axis=1, keepdims=True)) / norm
    grad_pooled = jnp.dot(grad_embed, out_weight.astype(jnp.float32).T, precision=HIGHEST)
    grad_heads = grad_pooled.reshape(images, heads, HEAD_DIM)
    grad_moments = jnp.einsum(
        "bhe,dhe->bhd", grad_heads, w_value.astype(jnp.float32), precision=HIGHEST
    ).astype(jnp.bfloat16)
    grad_attend = jnp.einsum(
        "bpd,bhd->bhp", patches, grad_moments, preferred_element_type=jnp.float32
    )
    grad_scores = attend * (grad_attend - jnp.sum(attend * grad_attend, axis=2, keepdims=True))
    key_moments = jnp.einsum(
        "bhp,bpd->hd",
        grad_scores.astype(jnp.bfloat16),
        patches,
        preferred_element_type=jnp.float32,
    )

    part = width // XS
    x_at = lax.axis_index("mp") % XS
    unit_part = lax.dynamic_slice_in_dim(unit, x_at * part, part, axis=1)
    for_texts = temper * jnp.sum(
        slope.reshape(images, dp, images)[..., None] * unit_part[:, None, None, :], axis=0
    )
    factors = jnp.concatenate([grad_pooled, pooled16.astype(jnp.float32)], axis=1)
    factors = jnp.broadcast_to(factors[None], (dp, images, 2 * local_width))
    sliced = jnp.concatenate(
        [moments16.astype(jnp.float32), grad_embed[:, None], key_moments[:, None]], axis=1
    )
    sliced = lax.optimization_barrier(sliced)
    sliced = (
        sliced.reshape(images, heads + 2, dp, rows)
        .transpose(2, 0, 1, 3)
        .reshape(dp, images, (heads + 2) * rows)
    )
    sent = jnp.concatenate([for_texts, factors, sliced], axis=2)
    used = sent.shape[2]
    sent = jnp.pad(sent, ((0, 0), (0, 0), (0, -used % 128)))
    got = lax.all_to_all(sent, "dp", 0, 0, tiled=True)

    text_part = jnp.sum(got[:, :, :part], axis=0)
    text_parts = spread(text_part, X_GROUPS, "mp")
    got_rows = got.reshape(total, sent.shape[2])
    at = part + 2 * local_width
    grads_all = got_rows[:, part : part + local_width].reshape(total, heads, HEAD_DIM)
    pooled_all = got_rows[:, part + local_width : at]
    moments_all = got_rows[:, at : at + heads * rows].reshape(total, heads, rows)
    columns_all = got_rows[:, at + heads * rows : used - rows]
    value_grad = jnp.einsum("bhd,bhe->dhe", moments_all, grads_all, precision=HIGHEST).reshape(
        rows, local_width
    )
    out_grad = jnp.dot(pooled_all.T, columns_all, precision=HIGHEST)
    key_sum = jnp.sum(got[:, :, used - rows : used], axis=0)
    key_grad = (key_sum.T[:, :, None] * q_heads[None] / head_root).reshape(rows, local_width)
    kv_grad = jnp.stack([key_grad, value_grad], axis=1)

    grad_txt = text_parts.transpose(1, 0, 2).reshape(images, width)
    own_text = texts.astype(jnp.float32)
    own_norm = jnp.sqrt(jnp.sum(own_text * own_text, axis=1, keepdims=True) + 1e-06)
    own_unit = own_text / own_norm
    text_grad = (
        grad_txt - own_unit * jnp.sum(own_unit * grad_txt, axis=1, keepdims=True)
    ) / own_norm
    return (kv_grad, out_grad, text_grad)


def solution(mesh):
    in_specs = (
        P("dp", None, None),
        P("dp"),
        P("dp"),
        P("dp", None),
        P(None, None, "mp"),
        P("mp", None),
        P("mp"),
        P(),
        P(),
    )
    out_specs = (P("dp", None, "mp"), P("mp", "dp"), P("dp", None))
    return jax.shard_map(local, mesh=mesh, in_specs=in_specs, out_specs=out_specs, check_vma=False)
```

```python
import math

import jax
import jax.numpy as jnp
from jax import lax
from jax.sharding import PartitionSpec as P

HEAD_DIM = 72
XS = 4
X_GROUPS = [list(range(XS)), list(range(XS, 2 * XS))]
HIGHEST = lax.Precision.HIGHEST


def spread(block, groups, axis, n):
    copies = jnp.broadcast_to(block[None], (n,) + block.shape)
    return lax.all_to_all(copies, axis, 0, 0, axis_index_groups=groups, tiled=True)


def halves(values):
    high = lax.reduce_precision(values, 8, 7)
    return jnp.concatenate([high, values - high], axis=-1).astype(jnp.bfloat16)


def whole(pairs):
    width = pairs.shape[-1] // 2
    pairs = pairs.astype(jnp.float32)
    return pairs[..., :width] + pairs[..., width:]


def local(patches, counts, pos_text, texts, kv_weight, out_weight, query, logit_scale, logit_bias):
    head_root = math.sqrt(HEAD_DIM)
    images, slot_count, width = patches.shape
    local_width = kv_weight.shape[2]
    heads = local_width // HEAD_DIM
    dp = lax.axis_size("dp")
    total = dp * images
    rows = width // dp
    temper = logit_scale[0]
    offset = logit_bias[0]

    text_all = spread(texts, None, "dp", dp)

    q_heads = query.reshape(heads, HEAD_DIM)
    w_key = kv_weight[:, 0, :].astype(jnp.float32).reshape(width, heads, HEAD_DIM)
    w_value = kv_weight[:, 1, :].reshape(width, heads, HEAD_DIM)
    probe = (jnp.einsum("dhe,he->dh", w_key, q_heads, precision=HIGHEST) / head_root).astype(
        jnp.bfloat16
    )
    live = (jnp.arange(slot_count, dtype=jnp.int32)[None, :] < counts[:, None])[:, None, :]
    scores = jnp.einsum("bpd,dh->bhp", patches, probe, preferred_element_type=jnp.float32)
    scores = jnp.where(live, scores, -1e30)
    peak = jnp.max(scores, axis=2, keepdims=True)
    raised = jnp.where(live, jnp.exp(scores - peak), 0.0)
    attend = raised / jnp.sum(raised, axis=2, keepdims=True)
    moments16 = jnp.einsum(
        "bhp,bpd->bhd", attend.astype(jnp.bfloat16), patches, preferred_element_type=jnp.float32
    ).astype(jnp.bfloat16)
    pooled16 = (
        jnp.einsum("bhd,dhe->bhe", moments16, w_value, preferred_element_type=jnp.float32)
        .reshape(images, local_width)
        .astype(jnp.bfloat16)
    )
    partial_value = jnp.dot(pooled16, out_weight, preferred_element_type=jnp.float32)

    along_x = lax.psum(partial_value, "mp", axis_index_groups=X_GROUPS)
    along_x, text_all = lax.optimization_barrier((along_x, text_all))
    mp = lax.axis_size("mp")
    embedding = along_x + lax.ppermute(
        along_x, "mp", [(i, (i + mp // 2) % mp) for i in range(mp)]
    )

    text_rows = text_all.reshape(total, width)
    text_f = text_rows.astype(jnp.float32)
    text_norm = jnp.sqrt(jnp.sum(text_f * text_f, axis=1) + 1e-06)
    text_unit = text_f / text_norm[:, None]

    norm = jnp.sqrt(jnp.sum(embedding * embedding, axis=1, keepdims=True) + 1e-06)
    unit = embedding / norm
    cosine = jnp.dot(unit, text_unit.T, precision=HIGHEST)
    columns = jnp.arange(total, dtype=jnp.int32)
    sign = jnp.where(pos_text[:, None] == columns[None, :], 1.0, -1.0)
    slope = -sign * jax.nn.sigmoid(-sign * (temper * cosine + offset))
    grad = temper * jnp.dot(slope, text_unit, precision=HIGHEST)
    grad_embed = (grad - unit * jnp.sum(unit * grad, axis=1, keepdims=True)) / norm
    grad_pooled = jnp.dot(grad_embed, out_weight.astype(jnp.float32).T, precision=HIGHEST)
    grad_heads = grad_pooled.reshape(images, heads, HEAD_DIM)
    grad_moments = jnp.einsum(
        "bhe,dhe->bhd", grad_heads, w_value.astype(jnp.float32), precision=HIGHEST
    ).astype(jnp.bfloat16)
    grad_attend = jnp.einsum(
        "bpd,bhd->bhp", patches, grad_moments, preferred_element_type=jnp.float32
    )
    grad_scores = attend * (grad_attend - jnp.sum(attend * grad_attend, axis=2, keepdims=True))
    key_moments = jnp.einsum(
        "bhp,bpd->hd",
        grad_scores.astype(jnp.bfloat16),
        patches,
        preferred_element_type=jnp.float32,
    )

    part = width // XS
    x_at = lax.axis_index("mp") % XS
    unit_part = lax.dynamic_slice_in_dim(unit, x_at * part, part, axis=1)
    for_texts = temper * jnp.sum(
        slope.reshape(images, dp, images)[..., None] * unit_part[:, None, None, :], axis=0
    )
    factors = jnp.concatenate([halves(grad_pooled), pooled16], axis=1)
    factors = jnp.broadcast_to(factors[None], (dp, images, 3 * local_width))
    sliced = jnp.concatenate([grad_embed[:, None], key_moments[:, None]], axis=1)
    high = lax.reduce_precision(sliced, 8, 7)
    sliced = jnp.concatenate(
        [moments16.astype(jnp.float32), high, sliced - high], axis=1
    )
    sliced = lax.optimization_barrier(sliced.astype(jnp.bfloat16))
    kinds = sliced.shape[1]
    sliced = (
        sliced.reshape(images, kinds, dp, rows)
        .transpose(2, 0, 1, 3)
        .reshape(dp, images, kinds * rows)
    )
    sent = jnp.concatenate([halves(for_texts), factors, sliced], axis=2)
    used = sent.shape[2]
    sent = jnp.pad(sent, ((0, 0), (0, 0), (0, -used % 128)))
    got = lax.all_to_all(sent, "dp", 0, 0, tiled=True)

    text_part = whole(jnp.sum(got[:, :, : 2 * part].astype(jnp.float32), axis=0))
    text_part, got = lax.optimization_barrier((text_part, got))
    text_parts = spread(text_part, X_GROUPS, "mp", XS)
    got_rows = got[:, :, 2 * part : used].astype(jnp.float32).reshape(total, used - 2 * part)
    at = 3 * local_width
    grads_all = whole(got_rows[:, : 2 * local_width]).reshape(total, heads, HEAD_DIM)
    pooled_all = got_rows[:, 2 * local_width : at]
    sliced_all = got_rows[:, at:].reshape(total, kinds, rows)
    moments_all = sliced_all[:, :heads]
    columns_all = sliced_all[:, heads] + sliced_all[:, heads + 2]
    key_sum = jnp.sum(
        (sliced_all[:, heads + 1] + sliced_all[:, heads + 3]).reshape(dp, images, rows), axis=0
    )
    value_grad = jnp.einsum("bhd,bhe->dhe", moments_all, grads_all, precision=HIGHEST).reshape(
        rows, local_width
    )
    out_grad = jnp.dot(pooled_all.T, columns_all, precision=HIGHEST)
    key_grad = (key_sum.T[:, :, None] * q_heads[None] / head_root).reshape(rows, local_width)
    kv_grad = jnp.stack([key_grad, value_grad], axis=1)

    grad_txt = text_parts.transpose(1, 0, 2).reshape(images, width)
    own_text = texts.astype(jnp.float32)
    own_norm = jnp.sqrt(jnp.sum(own_text * own_text, axis=1, keepdims=True) + 1e-06)
    own_unit = own_text / own_norm
    text_grad = (
        grad_txt - own_unit * jnp.sum(own_unit * grad_txt, axis=1, keepdims=True)
    ) / own_norm
    return (kv_grad, out_grad, text_grad)


def solution(mesh):
    in_specs = (
        P("dp", None, None),
        P("dp"),
        P("dp"),
        P("dp", None),
        P(None, None, "mp"),
        P("mp", None),
        P("mp"),
        P(),
        P(),
    )
    out_specs = (P("dp", None, "mp"), P("mp", "dp"), P("dp", None))
    return jax.shard_map(local, mesh=mesh, in_specs=in_specs, out_specs=out_specs, check_vma=False)
```

```python
import math

import jax
import jax.numpy as jnp
from jax import lax
from jax.sharding import PartitionSpec as P

HEAD_DIM = 72
XS = 4
X_GROUPS = [list(range(XS)), list(range(XS, 2 * XS))]
HIGHEST = lax.Precision.HIGHEST


def spread(block, groups, axis, n):
    copies = jnp.broadcast_to(block[None], (n,) + block.shape)
    return lax.all_to_all(copies, axis, 0, 0, axis_index_groups=groups, tiled=True)


def halves(values):
    high = lax.reduce_precision(values, 8, 7)
    return high, lax.reduce_precision(values - high, 8, 7)


def whole(pairs):
    width = pairs.shape[-1] // 2
    pairs = pairs.astype(jnp.float32)
    return pairs[..., :width] + pairs[..., width:]


def local(patches, counts, pos_text, texts, kv_weight, out_weight, query, logit_scale, logit_bias):
    head_root = math.sqrt(HEAD_DIM)
    images, slot_count, width = patches.shape
    local_width = kv_weight.shape[2]
    heads = local_width // HEAD_DIM
    dp = lax.axis_size("dp")
    total = dp * images
    rows = width // dp
    temper = logit_scale[0]
    offset = logit_bias[0]

    text_all = spread(texts, None, "dp", dp)

    q_heads = query.reshape(heads, HEAD_DIM)
    w_key = kv_weight[:, 0, :].astype(jnp.float32).reshape(width, heads, HEAD_DIM)
    w_value = kv_weight[:, 1, :].reshape(width, heads, HEAD_DIM)
    probe = (jnp.einsum("dhe,he->dh", w_key, q_heads, precision=HIGHEST) / head_root).astype(
        jnp.bfloat16
    )
    live = (jnp.arange(slot_count, dtype=jnp.int32)[None, :] < counts[:, None])[:, None, :]
    scores = jnp.einsum("bpd,dh->bhp", patches, probe, preferred_element_type=jnp.float32)
    scores = jnp.where(live, scores, -1e30)
    peak = jnp.max(scores, axis=2, keepdims=True)
    raised = jnp.where(live, jnp.exp(scores - peak), 0.0)
    attend = raised / jnp.sum(raised, axis=2, keepdims=True)
    moments16 = jnp.einsum(
        "bhp,bpd->bhd", attend.astype(jnp.bfloat16), patches, preferred_element_type=jnp.float32
    ).astype(jnp.bfloat16)
    pooled16 = (
        jnp.einsum("bhd,dhe->bhe", moments16, w_value, preferred_element_type=jnp.float32)
        .reshape(images, local_width)
        .astype(jnp.bfloat16)
    )
    partial_value = jnp.dot(pooled16, out_weight, preferred_element_type=jnp.float32)

    along_x = lax.psum(partial_value, "mp", axis_index_groups=X_GROUPS)
    along_x, text_all = lax.optimization_barrier((along_x, text_all))
    mp = lax.axis_size("mp")
    embedding = along_x + lax.ppermute(
        along_x, "mp", [(i, (i + mp // 2) % mp) for i in range(mp)]
    )

    text_rows = text_all.reshape(total, width)
    text_f = text_rows.astype(jnp.float32)
    text_norm = jnp.sqrt(jnp.sum(text_f * text_f, axis=1) + 1e-06)
    text_unit = text_f / text_norm[:, None]

    norm = jnp.sqrt(jnp.sum(embedding * embedding, axis=1, keepdims=True) + 1e-06)
    unit = embedding / norm
    cosine = jnp.dot(unit, text_unit.T, precision=HIGHEST)
    columns = jnp.arange(total, dtype=jnp.int32)
    sign = jnp.where(pos_text[:, None] == columns[None, :], 1.0, -1.0)
    slope = -sign * jax.nn.sigmoid(-sign * (temper * cosine + offset))
    grad = temper * jnp.dot(slope, text_unit, precision=HIGHEST)
    grad_embed = (grad - unit * jnp.sum(unit * grad, axis=1, keepdims=True)) / norm
    grad_pooled = jnp.dot(grad_embed, out_weight.astype(jnp.float32).T, precision=HIGHEST)
    grad_heads = grad_pooled.reshape(images, heads, HEAD_DIM)
    grad_moments = jnp.einsum(
        "bhe,dhe->bhd", grad_heads, w_value.astype(jnp.float32), precision=HIGHEST
    ).astype(jnp.bfloat16)
    grad_attend = jnp.einsum(
        "bpd,bhd->bhp", patches, grad_moments, preferred_element_type=jnp.float32
    )
    grad_scores = attend * (grad_attend - jnp.sum(attend * grad_attend, axis=2, keepdims=True))
    key_moments = jnp.einsum(
        "bhp,bpd->hd",
        grad_scores.astype(jnp.bfloat16),
        patches,
        preferred_element_type=jnp.float32,
    )

    part = width // XS
    half = part // 2
    core = lax.axis_index("dp") % 2
    x_at = lax.axis_index("mp") % XS * part
    unit_own = lax.dynamic_slice_in_dim(unit, x_at + core * half, half, axis=1)
    unit_other = lax.dynamic_slice_in_dim(unit, x_at + (1 - core) * half, half, axis=1)
    swapped = lax.ppermute(
        jnp.concatenate([slope, unit_other], axis=1), "dp", [(i, i ^ 1) for i in range(dp)]
    )
    key_moments, swapped = lax.optimization_barrier((key_moments, swapped))

    def outer(slopes, units):
        return jnp.sum(slopes.reshape(images, dp, images)[..., None] * units[:, None, None], axis=0)

    for_texts = temper * (outer(slope, unit_own) + outer(swapped[:, :total], swapped[:, total:]))
    text_high, text_low = halves(for_texts)
    grad_high, grad_low = halves(grad_pooled)
    factors = jnp.concatenate([grad_high, grad_low, pooled16.astype(jnp.float32)], axis=1)
    sliced = jnp.concatenate([grad_embed[:, None], key_moments[:, None]], axis=1)
    sliced = jnp.concatenate([moments16.astype(jnp.float32), *halves(sliced)], axis=1)
    sliced = lax.optimization_barrier(sliced)
    kinds = sliced.shape[1]
    sliced = (
        sliced.reshape(images, kinds, dp, rows)
        .transpose(2, 0, 1, 3)
        .reshape(dp, images, kinds * rows)
    )
    factor_at = 2 * half
    slice_at = factor_at + 3 * local_width
    used = slice_at + kinds * rows
    size = used + -used % 128

    def place(values, at):
        return jnp.pad(values, ((0, 0), (0, 0), (at, size - at - values.shape[2])))

    sent = (
        place(text_high, 0)
        + place(text_low, half)
        + place(factors[None], factor_at)
        + place(sliced, slice_at)
    ).astype(jnp.bfloat16)
    got = lax.all_to_all(sent, "dp", 0, 0, tiled=True)

    text_sums = jnp.sum(
        got[:, :, :factor_at].astype(jnp.float32).reshape(dp // 2, 2, images, factor_at), axis=0
    )
    text_part = (text_sums[..., :half] + text_sums[..., half:]).transpose(1, 0, 2)
    text_part = text_part.reshape(images, part)
    text_part, got = lax.optimization_barrier((text_part, got))
    text_parts = spread(text_part, X_GROUPS, "mp", XS)
    got_rows = got[:, :, factor_at:used].astype(jnp.float32).reshape(total, used - factor_at)
    at = 3 * local_width
    grads_all = whole(got_rows[:, : 2 * local_width]).reshape(total, heads, HEAD_DIM)
    pooled_all = got_rows[:, 2 * local_width : at]
    sliced_all = got_rows[:, at:].reshape(total, kinds, rows)
    moments_all = sliced_all[:, :heads]
    columns_all = sliced_all[:, heads] + sliced_all[:, heads + 2]
    key_sum = jnp.sum(
        (sliced_all[:, heads + 1] + sliced_all[:, heads + 3]).reshape(dp, images, rows), axis=0
    )
    value_grad = jnp.einsum("bhd,bhe->dhe", moments_all, grads_all, precision=HIGHEST).reshape(
        rows, local_width
    )
    out_grad = jnp.dot(pooled_all.T, columns_all, precision=HIGHEST)
    key_grad = (key_sum.T[:, :, None] * q_heads[None] / head_root).reshape(rows, local_width)
    kv_grad = jnp.stack([key_grad, value_grad], axis=1)

    grad_txt = text_parts.transpose(1, 0, 2).reshape(images, width)
    own_text = texts.astype(jnp.float32)
    own_norm = jnp.sqrt(jnp.sum(own_text * own_text, axis=1, keepdims=True) + 1e-06)
    own_unit = own_text / own_norm
    text_grad = (
        grad_txt - own_unit * jnp.sum(own_unit * grad_txt, axis=1, keepdims=True)
    ) / own_norm
    return (kv_grad, out_grad, text_grad)


def solution(mesh):
    in_specs = (
        P("dp", None, None),
        P("dp"),
        P("dp"),
        P("dp", None),
        P(None, None, "mp"),
        P("mp", None),
        P("mp"),
        P(),
        P(),
    )
    out_specs = (P("dp", None, "mp"), P("mp", "dp"), P("dp", None))
    return jax.shard_map(local, mesh=mesh, in_specs=in_specs, out_specs=out_specs, check_vma=False)
```

```python
import math

import jax
import jax.numpy as jnp
from jax import lax
from jax.sharding import PartitionSpec as P

HEAD_DIM = 72
ZL, YC = 6, 16
ZL_GROUPS = [[z * YC + r for z in range(ZL)] for r in range(YC)]
YC_GROUPS = [[z * YC + r for r in range(YC)] for z in range(ZL)]
XS = 4
X_GROUPS = [list(range(XS)), list(range(XS, 2 * XS))]
HIGHEST = lax.Precision.HIGHEST


def spread(block, groups, axis, n):
    copies = jnp.broadcast_to(block[None], (n,) + block.shape)
    return lax.all_to_all(copies, axis, 0, 0, axis_index_groups=groups, tiled=True)


def halves(values):
    high = lax.reduce_precision(values, 8, 7)
    return high, lax.reduce_precision(values - high, 8, 7)


def local(patches, counts, pos_text, texts, kv_weight, out_weight, query, logit_scale, logit_bias):
    head_root = math.sqrt(HEAD_DIM)
    images, slot_count, width = patches.shape
    local_width = kv_weight.shape[2]
    heads = local_width // HEAD_DIM
    dp = lax.axis_size("dp")
    total = dp * images
    rows = width // dp
    temper = logit_scale[0]
    offset = logit_bias[0]

    text_all = spread(texts, None, "dp", dp)

    q_heads = query.reshape(heads, HEAD_DIM)
    w_key = kv_weight[:, 0, :].astype(jnp.float32).reshape(width, heads, HEAD_DIM)
    w_value = kv_weight[:, 1, :].reshape(width, heads, HEAD_DIM)
    probe = (jnp.einsum("dhe,he->dh", w_key, q_heads, precision=HIGHEST) / head_root).astype(
        jnp.bfloat16
    )
    live = (jnp.arange(slot_count, dtype=jnp.int32)[None, :] < counts[:, None])[:, None, :]
    scores = jnp.einsum("bpd,dh->bhp", patches, probe, preferred_element_type=jnp.float32)
    scores = jnp.where(live, scores, -1e30)
    peak = jnp.max(scores, axis=2, keepdims=True)
    raised = jnp.where(live, jnp.exp(scores - peak), 0.0)
    attend = raised / jnp.sum(raised, axis=2, keepdims=True)
    moments16 = jnp.einsum(
        "bhp,bpd->bhd", attend.astype(jnp.bfloat16), patches, preferred_element_type=jnp.float32
    ).astype(jnp.bfloat16)
    pooled16 = (
        jnp.einsum("bhd,dhe->bhe", moments16, w_value, preferred_element_type=jnp.float32)
        .reshape(images, local_width)
        .astype(jnp.bfloat16)
    )
    partial_value = jnp.dot(pooled16, out_weight, preferred_element_type=jnp.float32)

    along_x = lax.psum(partial_value, "mp", axis_index_groups=X_GROUPS)
    along_x, text_all = lax.optimization_barrier((along_x, text_all))
    mp = lax.axis_size("mp")
    embedding = along_x + lax.ppermute(
        along_x, "mp", [(i, (i + mp // 2) % mp) for i in range(mp)]
    )

    text_rows = text_all.reshape(total, width)
    text_f = text_rows.astype(jnp.float32)
    text_norm = jnp.sqrt(jnp.sum(text_f * text_f, axis=1) + 1e-06)
    text_unit = text_f / text_norm[:, None]

    norm = jnp.sqrt(jnp.sum(embedding * embedding, axis=1, keepdims=True) + 1e-06)
    unit = embedding / norm
    cosine = jnp.dot(unit, text_unit.T, precision=HIGHEST)
    columns = jnp.arange(total, dtype=jnp.int32)
    sign = jnp.where(pos_text[:, None] == columns[None, :], 1.0, -1.0)
    slope = -sign * jax.nn.sigmoid(-sign * (temper * cosine + offset))
    grad = temper * jnp.dot(slope, text_unit, precision=HIGHEST)
    grad_embed = (grad - unit * jnp.sum(unit * grad, axis=1, keepdims=True)) / norm
    grad_pooled = jnp.dot(grad_embed, out_weight.astype(jnp.float32).T, precision=HIGHEST)
    grad_heads = grad_pooled.reshape(images, heads, HEAD_DIM)
    grad_moments = jnp.einsum(
        "bhe,dhe->bhd", grad_heads, w_value.astype(jnp.float32), precision=HIGHEST
    ).astype(jnp.bfloat16)
    grad_attend = jnp.einsum(
        "bpd,bhd->bhp", patches, grad_moments, preferred_element_type=jnp.float32
    )
    grad_scores = attend * (grad_attend - jnp.sum(attend * grad_attend, axis=2, keepdims=True))
    key_moments = jnp.einsum(
        "bhp,bpd->hd",
        grad_scores.astype(jnp.bfloat16),
        patches,
        preferred_element_type=jnp.float32,
    )

    part = width // XS
    half = part // 2
    core = lax.axis_index("dp") % 2
    x_at = lax.axis_index("mp") % XS * part
    unit_own = lax.dynamic_slice_in_dim(unit, x_at + core * half, half, axis=1)
    unit_other = lax.dynamic_slice_in_dim(unit, x_at + (1 - core) * half, half, axis=1)
    swapped = lax.ppermute(
        jnp.concatenate([slope, unit_other], axis=1), "dp", [(i, i ^ 1) for i in range(dp)]
    )
    key_moments, swapped = lax.optimization_barrier((key_moments, swapped))

    def outer(slopes, units):
        return jnp.sum(slopes.reshape(images, dp, images)[..., None] * units[:, None, None], axis=0)

    for_texts = temper * (outer(slope, unit_own) + outer(swapped[:, :total], swapped[:, total:]))
    text_high, text_low = halves(for_texts)
    grad_high, grad_low = halves(grad_pooled)
    factors = jnp.concatenate([grad_high, grad_low, pooled16.astype(jnp.float32)], axis=1)
    sliced = jnp.stack([*halves(grad_embed), *halves(key_moments)], axis=1)
    sliced = jnp.concatenate([moments16.astype(jnp.float32), sliced], axis=1)
    sliced = lax.optimization_barrier(sliced)
    kinds = sliced.shape[1]
    sliced = (
        sliced.reshape(images, kinds, dp, rows)
        .transpose(2, 0, 1, 3)
        .reshape(dp, images, kinds * rows)
    )

    def place(values, at, size):
        rest = ((0, 0),) * (values.ndim - 1)
        return jnp.pad(values, rest + ((at, size - at - values.shape[-1]),))

    slice_at = 2 * half
    key_at = slice_at + (kinds - 2) * rows
    used = slice_at + kinds * rows
    size = used + -used % 128
    cut = 3 * local_width // 2
    rows_sent = place(text_high, 0, size) + place(text_low, half, size)
    rows_sent = (rows_sent + place(sliced, slice_at, size)).reshape(ZL, YC, images, size)
    factors = place(jnp.stack([factors[:, :cut], factors[:, cut:]]), 0, size)
    factors = jnp.broadcast_to(factors[None], (ZL,) + factors.shape)
    sent = jnp.concatenate([rows_sent, factors], axis=1).astype(jnp.bfloat16)
    got = lax.all_to_all(sent, "dp", 0, 0, axis_index_groups=ZL_GROUPS, tiled=True)
    got = got.astype(jnp.float32)

    sums = jnp.sum(got[:, :YC], axis=0)
    text_sum = halves(sums[..., :half] + sums[..., half:slice_at])
    key_sum = halves(sums[..., key_at : key_at + rows] + sums[..., key_at + rows : used])
    wide = 3 * local_width + key_at - slice_at
    wide = wide + -wide % 128
    sums_sent = place(text_sum[0], 0, wide) + place(text_sum[1], half, wide)
    sums_sent = sums_sent + place(key_sum[0], slice_at, wide)
    sums_sent = (sums_sent + place(key_sum[1], slice_at + rows, wide))[:, None]
    rows_all = got[:, :YC, :, slice_at:key_at].transpose(1, 0, 2, 3)
    factors = place(got[:, YC, :, :cut], 0, wide) + place(got[:, YC + 1, :, :cut], cut, wide)
    factors = factors[None] + place(rows_all, 3 * local_width, wide)
    sent = jnp.concatenate([factors, sums_sent], axis=1).astype(jnp.bfloat16)
    got = lax.all_to_all(sent, "dp", 0, 0, axis_index_groups=YC_GROUPS, tiled=True)

    text_sums = got[:, ZL].astype(jnp.float32).reshape(YC // 2, 2, images, wide)
    text_sums = jnp.sum(text_sums, axis=0)
    text_part = (text_sums[..., :half] + text_sums[..., half:slice_at]).transpose(1, 0, 2)
    text_part = text_part.reshape(images, part)
    text_part, text_sums, got = lax.optimization_barrier((text_part, text_sums, got))
    text_parts = spread(text_part, X_GROUPS, "mp", XS)
    key_sum = jnp.sum(text_sums[..., slice_at : slice_at + 2 * rows], axis=0)
    key_sum = key_sum[:, :rows] + key_sum[:, rows:]
    got_rows = got[:, :ZL].astype(jnp.float32).reshape(total, wide)
    at = 3 * local_width
    grads_all = got_rows[:, :local_width] + got_rows[:, local_width : 2 * local_width]
    grads_all = grads_all.reshape(total, heads, HEAD_DIM)
    pooled_all = got_rows[:, 2 * local_width : at]
    moments_all = got_rows[:, at : at + heads * rows].reshape(total, heads, rows)
    at = at + heads * rows
    columns_all = got_rows[:, at : at + rows] + got_rows[:, at + rows : at + 2 * rows]
    value_grad = jnp.einsum("bhd,bhe->dhe", moments_all, grads_all, precision=HIGHEST).reshape(
        rows, local_width
    )
    out_grad = jnp.dot(pooled_all.T, columns_all, precision=HIGHEST)
    key_grad = (key_sum.T[:, :, None] * q_heads[None] / head_root).reshape(rows, local_width)
    kv_grad = jnp.stack([key_grad, value_grad], axis=1)

    grad_txt = text_parts.transpose(1, 0, 2).reshape(images, width)
    own_text = texts.astype(jnp.float32)
    own_norm = jnp.sqrt(jnp.sum(own_text * own_text, axis=1, keepdims=True) + 1e-06)
    own_unit = own_text / own_norm
    text_grad = (
        grad_txt - own_unit * jnp.sum(own_unit * grad_txt, axis=1, keepdims=True)
    ) / own_norm
    return (kv_grad, out_grad, text_grad)


def solution(mesh):
    in_specs = (
        P("dp", None, None),
        P("dp"),
        P("dp"),
        P("dp", None),
        P(None, None, "mp"),
        P("mp", None),
        P("mp"),
        P(),
        P(),
    )
    out_specs = (P("dp", None, "mp"), P("mp", "dp"), P("dp", None))
    return jax.shard_map(local, mesh=mesh, in_specs=in_specs, out_specs=out_specs, check_vma=False)
```

```python
import math

import jax
import jax.numpy as jnp
from jax import lax
from jax.sharding import PartitionSpec as P

HEAD_DIM = 72
XS = 4
X_GROUPS = [list(range(XS)), list(range(XS, 2 * XS))]
HIGHEST = lax.Precision.HIGHEST


def spread(block, groups, axis, n):
    copies = jnp.broadcast_to(block[None], (n,) + block.shape)
    return lax.all_to_all(copies, axis, 0, 0, axis_index_groups=groups, tiled=True)


def halves(values):
    high = lax.reduce_precision(values, 8, 7)
    return high, lax.reduce_precision(values - high, 8, 7)


def whole(pairs):
    width = pairs.shape[-1] // 2
    pairs = pairs.astype(jnp.float32)
    return pairs[..., :width] + pairs[..., width:]


def local(patches, counts, pos_text, texts, kv_weight, out_weight, query, logit_scale, logit_bias):
    head_root = math.sqrt(HEAD_DIM)
    images, slot_count, width = patches.shape
    local_width = kv_weight.shape[2]
    heads = local_width // HEAD_DIM
    dp = lax.axis_size("dp")
    total = dp * images
    rows = width // dp
    temper = logit_scale[0]
    offset = logit_bias[0]

    core = lax.axis_index("dp") % 2
    swap = [(i, i ^ 1) for i in range(dp)]
    text_same = spread(texts, [list(range(c, dp, 2)) for c in range(2)], "dp", dp // 2)

    q_heads = query.reshape(heads, HEAD_DIM)
    w_key = kv_weight[:, 0, :].astype(jnp.float32).reshape(width, heads, HEAD_DIM)
    w_value = kv_weight[:, 1, :].reshape(width, heads, HEAD_DIM)
    probe = (jnp.einsum("dhe,he->dh", w_key, q_heads, precision=HIGHEST) / head_root).astype(
        jnp.bfloat16
    )
    live = (jnp.arange(slot_count, dtype=jnp.int32)[None, :] < counts[:, None])[:, None, :]
    scores = jnp.einsum("bpd,dh->bhp", patches, probe, preferred_element_type=jnp.float32)
    scores = jnp.where(live, scores, -1e30)
    peak = jnp.max(scores, axis=2, keepdims=True)
    raised = jnp.where(live, jnp.exp(scores - peak), 0.0)
    attend = raised / jnp.sum(raised, axis=2, keepdims=True)
    moments16 = jnp.einsum(
        "bhp,bpd->bhd", attend.astype(jnp.bfloat16), patches, preferred_element_type=jnp.float32
    ).astype(jnp.bfloat16)
    pooled16 = (
        jnp.einsum("bhd,dhe->bhe", moments16, w_value, preferred_element_type=jnp.float32)
        .reshape(images, local_width)
        .astype(jnp.bfloat16)
    )
    partial_value = jnp.dot(pooled16, out_weight, preferred_element_type=jnp.float32)

    partial_value, text_same = lax.optimization_barrier((partial_value, text_same))
    text_other = lax.ppermute(text_same, "dp", swap)
    along_x = lax.psum(partial_value, "mp", axis_index_groups=X_GROUPS)
    along_x, text_other = lax.optimization_barrier((along_x, text_other))
    mp = lax.axis_size("mp")
    embedding = along_x + lax.ppermute(
        along_x, "mp", [(i, (i + mp // 2) % mp) for i in range(mp)]
    )

    text_rows = jnp.concatenate([text_same, text_other], axis=0).reshape(total, width)
    text_f = text_rows.astype(jnp.float32)
    text_norm = jnp.sqrt(jnp.sum(text_f * text_f, axis=1) + 1e-06)
    text_unit = text_f / text_norm[:, None]

    norm = jnp.sqrt(jnp.sum(embedding * embedding, axis=1, keepdims=True) + 1e-06)
    unit = embedding / norm
    cosine = jnp.dot(unit, text_unit.T, precision=HIGHEST)
    columns = jnp.arange(total, dtype=jnp.int32)
    chip = columns % (total // 2) // images
    owner = 2 * chip + jnp.where(columns < total // 2, core, 1 - core)
    columns = owner * images + columns % images
    sign = jnp.where(pos_text[:, None] == columns[None, :], 1.0, -1.0)
    slope = -sign * jax.nn.sigmoid(-sign * (temper * cosine + offset))
    grad = temper * jnp.dot(slope, text_unit, precision=HIGHEST)
    grad_embed = (grad - unit * jnp.sum(unit * grad, axis=1, keepdims=True)) / norm
    grad_pooled = jnp.dot(grad_embed, out_weight.astype(jnp.float32).T, precision=HIGHEST)
    grad_heads = grad_pooled.reshape(images, heads, HEAD_DIM)
    grad_moments = jnp.einsum(
        "bhe,dhe->bhd", grad_heads, w_value.astype(jnp.float32), precision=HIGHEST
    ).astype(jnp.bfloat16)
    grad_attend = jnp.einsum(
        "bpd,bhd->bhp", patches, grad_moments, preferred_element_type=jnp.float32
    )
    grad_scores = attend * (grad_attend - jnp.sum(attend * grad_attend, axis=2, keepdims=True))
    key_moments = jnp.einsum(
        "bhp,bpd->hd",
        grad_scores.astype(jnp.bfloat16),
        patches,
        preferred_element_type=jnp.float32,
    )

    same, other = slope[:, : total // 2], slope[:, total // 2 :]
    by_core = [jnp.where(core == c, same, other).reshape(images, dp // 2, images) for c in range(2)]
    slope = jnp.stack(by_core, axis=2).reshape(images, total)
    part = width // XS
    half = part // 2
    x_at = lax.axis_index("mp") % XS * part
    unit_own = lax.dynamic_slice_in_dim(unit, x_at + core * half, half, axis=1)
    unit_other = lax.dynamic_slice_in_dim(unit, x_at + (1 - core) * half, half, axis=1)
    swapped = lax.ppermute(
        jnp.concatenate([slope, unit_other], axis=1), "dp", swap
    )
    key_moments, swapped = lax.optimization_barrier((key_moments, swapped))

    def outer(slopes, units):
        return jnp.sum(slopes.reshape(images, dp, images)[..., None] * units[:, None, None], axis=0)

    for_texts = temper * (outer(slope, unit_own) + outer(swapped[:, :total], swapped[:, total:]))
    text_high, text_low = halves(for_texts)
    grad_high, grad_low = halves(grad_pooled)
    factors = jnp.concatenate([grad_high, grad_low, pooled16.astype(jnp.float32)], axis=1)
    sliced = jnp.concatenate([grad_embed[:, None], key_moments[:, None]], axis=1)
    sliced = jnp.concatenate([moments16.astype(jnp.float32), *halves(sliced)], axis=1)
    sliced = lax.optimization_barrier(sliced)
    kinds = sliced.shape[1]
    sliced = (
        sliced.reshape(images, kinds, dp, rows)
        .transpose(2, 0, 1, 3)
        .reshape(dp, images, kinds * rows)
    )
    factor_at = 2 * half
    slice_at = factor_at + 3 * local_width
    used = slice_at + kinds * rows
    size = used + -used % 128

    def place(values, at):
        return jnp.pad(values, ((0, 0), (0, 0), (at, size - at - values.shape[2])))

    sent = (
        place(text_high, 0)
        + place(text_low, half)
        + place(factors[None], factor_at)
        + place(sliced, slice_at)
    ).astype(jnp.bfloat16)
    got = lax.all_to_all(sent, "dp", 0, 0, tiled=True)

    text_sums = jnp.sum(
        got[:, :, :factor_at].astype(jnp.float32).reshape(dp // 2, 2, images, factor_at), axis=0
    )
    text_part = (text_sums[..., :half] + text_sums[..., half:]).transpose(1, 0, 2)
    text_part = text_part.reshape(images, part)
    text_part, got = lax.optimization_barrier((text_part, got))
    text_parts = spread(text_part, X_GROUPS, "mp", XS)
    got_rows = got[:, :, factor_at:used].astype(jnp.float32).reshape(total, used - factor_at)
    at = 3 * local_width
    grads_all = whole(got_rows[:, : 2 * local_width]).reshape(total, heads, HEAD_DIM)
    pooled_all = got_rows[:, 2 * local_width : at]
    sliced_all = got_rows[:, at:].reshape(total, kinds, rows)
    moments_all = sliced_all[:, :heads]
    columns_all = sliced_all[:, heads] + sliced_all[:, heads + 2]
    key_sum = jnp.sum(
        (sliced_all[:, heads + 1] + sliced_all[:, heads + 3]).reshape(dp, images, rows), axis=0
    )
    value_grad = jnp.einsum("bhd,bhe->dhe", moments_all, grads_all, precision=HIGHEST).reshape(
        rows, local_width
    )
    out_grad = jnp.dot(pooled_all.T, columns_all, precision=HIGHEST)
    key_grad = (key_sum.T[:, :, None] * q_heads[None] / head_root).reshape(rows, local_width)
    kv_grad = jnp.stack([key_grad, value_grad], axis=1)

    grad_txt = text_parts.transpose(1, 0, 2).reshape(images, width)
    own_text = texts.astype(jnp.float32)
    own_norm = jnp.sqrt(jnp.sum(own_text * own_text, axis=1, keepdims=True) + 1e-06)
    own_unit = own_text / own_norm
    text_grad = (
        grad_txt - own_unit * jnp.sum(own_unit * grad_txt, axis=1, keepdims=True)
    ) / own_norm
    return (kv_grad, out_grad, text_grad)


def solution(mesh):
    in_specs = (
        P("dp", None, None),
        P("dp"),
        P("dp"),
        P("dp", None),
        P(None, None, "mp"),
        P("mp", None),
        P("mp"),
        P(),
        P(),
    )
    out_specs = (P("dp", None, "mp"), P("mp", "dp"), P("dp", None))
    return jax.shard_map(local, mesh=mesh, in_specs=in_specs, out_specs=out_specs, check_vma=False)
```

```python
import math

import jax
import jax.numpy as jnp
from jax import lax
from jax.sharding import PartitionSpec as P

HEAD_DIM = 72
XS = 4
X_GROUPS = [list(range(XS)), list(range(XS, 2 * XS))]
HIGHEST = lax.Precision.HIGHEST


def spread(block, groups, axis, n):
    copies = jnp.broadcast_to(block[None], (n,) + block.shape)
    return lax.all_to_all(copies, axis, 0, 0, axis_index_groups=groups, tiled=True)


def halves(values):
    high = lax.reduce_precision(values, 8, 7)
    return high, lax.reduce_precision(values - high, 8, 7)


def whole(pairs):
    width = pairs.shape[-1] // 2
    pairs = pairs.astype(jnp.float32)
    return pairs[..., :width] + pairs[..., width:]


def local(patches, counts, pos_text, texts, kv_weight, out_weight, query, logit_scale, logit_bias):
    head_root = math.sqrt(HEAD_DIM)
    images, slot_count, width = patches.shape
    local_width = kv_weight.shape[2]
    heads = local_width // HEAD_DIM
    dp = lax.axis_size("dp")
    total = dp * images
    rows = width // dp
    temper = logit_scale[0]
    offset = logit_bias[0]

    text_all = spread(texts, None, "dp", dp)

    q_heads = query.reshape(heads, HEAD_DIM)
    w_key = kv_weight[:, 0, :].astype(jnp.float32).reshape(width, heads, HEAD_DIM)
    w_value = kv_weight[:, 1, :].reshape(width, heads, HEAD_DIM)
    probe = (jnp.einsum("dhe,he->dh", w_key, q_heads, precision=HIGHEST) / head_root).astype(
        jnp.bfloat16
    )
    live = (jnp.arange(slot_count, dtype=jnp.int32)[None, :] < counts[:, None])[:, None, :]
    scores = jnp.einsum("bpd,dh->bhp", patches, probe, preferred_element_type=jnp.float32)
    scores = jnp.where(live, scores, -1e30)
    peak = jnp.max(scores, axis=2, keepdims=True)
    raised = jnp.where(live, jnp.exp(scores - peak), 0.0)
    attend = raised / jnp.sum(raised, axis=2, keepdims=True)
    moments16 = jnp.einsum(
        "bhp,bpd->bhd", attend.astype(jnp.bfloat16), patches, preferred_element_type=jnp.float32
    ).astype(jnp.bfloat16)
    pooled16 = (
        jnp.einsum("bhd,dhe->bhe", moments16, w_value, preferred_element_type=jnp.float32)
        .reshape(images, local_width)
        .astype(jnp.bfloat16)
    )
    partial_value = jnp.dot(pooled16, out_weight, preferred_element_type=jnp.float32)

    along_x = lax.psum(partial_value, "mp", axis_index_groups=X_GROUPS)
    along_x, text_all = lax.optimization_barrier((along_x, text_all))
    mp = lax.axis_size("mp")
    embedding = along_x + lax.ppermute(
        along_x, "mp", [(i, (i + mp // 2) % mp) for i in range(mp)]
    )

    text_rows = text_all.reshape(total, width)
    text_f = text_rows.astype(jnp.float32)
    text_norm = jnp.sqrt(jnp.sum(text_f * text_f, axis=1) + 1e-06)
    text_unit = text_f / text_norm[:, None]

    norm = jnp.sqrt(jnp.sum(embedding * embedding, axis=1, keepdims=True) + 1e-06)
    unit = embedding / norm
    cosine = jnp.dot(unit, text_unit.T, precision=HIGHEST)
    columns = jnp.arange(total, dtype=jnp.int32)
    sign = jnp.where(pos_text[:, None] == columns[None, :], 1.0, -1.0)
    slope = -sign * jax.nn.sigmoid(-sign * (temper * cosine + offset))
    grad = temper * jnp.dot(slope, text_unit, precision=HIGHEST)
    grad_embed = (grad - unit * jnp.sum(unit * grad, axis=1, keepdims=True)) / norm
    grad_pooled = jnp.dot(grad_embed, out_weight.astype(jnp.float32).T, precision=HIGHEST)
    grad_heads = grad_pooled.reshape(images, heads, HEAD_DIM)
    grad_moments = jnp.einsum(
        "bhe,dhe->bhd", grad_heads, w_value.astype(jnp.float32), precision=HIGHEST
    ).astype(jnp.bfloat16)
    grad_attend = jnp.einsum(
        "bpd,bhd->bhp", patches, grad_moments, preferred_element_type=jnp.float32
    )
    grad_scores = attend * (grad_attend - jnp.sum(attend * grad_attend, axis=2, keepdims=True))
    key_moments = jnp.einsum(
        "bhp,bpd->hd",
        grad_scores.astype(jnp.bfloat16),
        patches,
        preferred_element_type=jnp.float32,
    )

    part = width // XS
    half = part // 2
    core = lax.axis_index("dp") % 2
    x_at = lax.axis_index("mp") % XS * part
    unit_own = lax.dynamic_slice_in_dim(unit, x_at + core * half, half, axis=1)
    unit_other = lax.dynamic_slice_in_dim(unit, x_at + (1 - core) * half, half, axis=1)
    swapped = lax.ppermute(
        jnp.concatenate([slope, unit_other], axis=1), "dp", [(i, i ^ 1) for i in range(dp)]
    )
    key_moments, swapped = lax.optimization_barrier((key_moments, swapped))

    slopes = jnp.concatenate([slope, swapped[:, :total]], axis=0)
    units = jnp.concatenate([unit_own, swapped[:, total:]], axis=0)
    for_texts = temper * lax.dot_general(
        slopes, units, (((0,), (0,)), ((), ())), precision=HIGHEST
    ).reshape(dp, images, half)
    text_high, text_low = halves(for_texts)
    grad_high, grad_low = halves(grad_pooled)
    factors = jnp.concatenate([grad_high, grad_low, pooled16.astype(jnp.float32)], axis=1)
    sliced = jnp.concatenate([grad_embed[:, None], key_moments[:, None]], axis=1)
    sliced = jnp.concatenate([moments16.astype(jnp.float32), *halves(sliced)], axis=1)
    sliced = lax.optimization_barrier(sliced)
    kinds = sliced.shape[1]
    sliced = (
        sliced.reshape(images, kinds, dp, rows)
        .transpose(2, 0, 1, 3)
        .reshape(dp, images, kinds * rows)
    )
    factor_at = 2 * half
    slice_at = factor_at + 3 * local_width
    used = slice_at + kinds * rows
    size = used + -used % 128

    def place(values, at):
        return jnp.pad(values, ((0, 0), (0, 0), (at, size - at - values.shape[2])))

    sent = (
        place(text_high, 0)
        + place(text_low, half)
        + place(factors[None], factor_at)
        + place(sliced, slice_at)
    ).astype(jnp.bfloat16)
    got = lax.all_to_all(sent, "dp", 0, 0, tiled=True)

    text_sums = jnp.sum(
        got[:, :, :factor_at].astype(jnp.float32).reshape(dp // 2, 2, images, factor_at), axis=0
    )
    text_part = (text_sums[..., :half] + text_sums[..., half:]).transpose(1, 0, 2)
    text_part = text_part.reshape(images, part)
    text_part, got = lax.optimization_barrier((text_part, got))
    text_parts = spread(text_part, X_GROUPS, "mp", XS)
    got_rows = got[:, :, factor_at:used].astype(jnp.float32).reshape(total, used - factor_at)
    at = 3 * local_width
    grads_all = whole(got_rows[:, : 2 * local_width]).reshape(total, heads, HEAD_DIM)
    pooled_all = got_rows[:, 2 * local_width : at]
    sliced_all = got_rows[:, at:].reshape(total, kinds, rows)
    moments_all = sliced_all[:, :heads]
    columns_all = sliced_all[:, heads] + sliced_all[:, heads + 2]
    key_sum = jnp.sum(
        (sliced_all[:, heads + 1] + sliced_all[:, heads + 3]).reshape(dp, images, rows), axis=0
    )
    value_grad = jnp.einsum("bhd,bhe->dhe", moments_all, grads_all, precision=HIGHEST).reshape(
        rows, local_width
    )
    out_grad = jnp.dot(pooled_all.T, columns_all, precision=HIGHEST)
    key_grad = (key_sum.T[:, :, None] * q_heads[None] / head_root).reshape(rows, local_width)
    kv_grad = jnp.stack([key_grad, value_grad], axis=1)

    grad_txt = text_parts.transpose(1, 0, 2).reshape(images, width)
    own_text = texts.astype(jnp.float32)
    own_norm = jnp.sqrt(jnp.sum(own_text * own_text, axis=1, keepdims=True) + 1e-06)
    own_unit = own_text / own_norm
    text_grad = (
        grad_txt - own_unit * jnp.sum(own_unit * grad_txt, axis=1, keepdims=True)
    ) / own_norm
    return (kv_grad, out_grad, text_grad)


def solution(mesh):
    in_specs = (
        P("dp", None, None),
        P("dp"),
        P("dp"),
        P("dp", None),
        P(None, None, "mp"),
        P("mp", None),
        P("mp"),
        P(),
        P(),
    )
    out_specs = (P("dp", None, "mp"), P("mp", "dp"), P("dp", None))
    return jax.shard_map(local, mesh=mesh, in_specs=in_specs, out_specs=out_specs, check_vma=False)
```

```python
import math

import jax
import jax.numpy as jnp
from jax import lax
from jax.sharding import PartitionSpec as P

HEAD_DIM = 72
XS = 4
X_GROUPS = [list(range(XS)), list(range(XS, 2 * XS))]
HIGHEST = lax.Precision.HIGHEST


def spread(block, groups, axis, n):
    copies = jnp.broadcast_to(block[None], (n,) + block.shape)
    return lax.all_to_all(copies, axis, 0, 0, axis_index_groups=groups, tiled=True)


def halves(values):
    high = lax.reduce_precision(values, 8, 7)
    return high, lax.reduce_precision(values - high, 8, 7)


def whole(pairs):
    width = pairs.shape[-1] // 2
    pairs = pairs.astype(jnp.float32)
    return pairs[..., :width] + pairs[..., width:]


def local(patches, counts, pos_text, texts, kv_weight, out_weight, query, logit_scale, logit_bias):
    head_root = math.sqrt(HEAD_DIM)
    images, slot_count, width = patches.shape
    local_width = kv_weight.shape[2]
    heads = local_width // HEAD_DIM
    dp = lax.axis_size("dp")
    total = dp * images
    rows = width // dp
    temper = logit_scale[0]
    offset = logit_bias[0]

    text_all = spread(texts, None, "dp", dp)

    q_heads = query.reshape(heads, HEAD_DIM)
    w_key = kv_weight[:, 0, :].astype(jnp.float32)
    own_head = jnp.arange(local_width)[:, None] // HEAD_DIM == jnp.arange(heads)[None, :]
    q_blocks = jnp.where(own_head, query[:, None], 0.0)
    w_value = kv_weight[:, 1, :].reshape(width, heads, HEAD_DIM)
    probe = (jnp.dot(w_key, q_blocks, precision=HIGHEST) / head_root).astype(
        jnp.bfloat16
    )
    live = (jnp.arange(slot_count, dtype=jnp.int32)[None, :] < counts[:, None])[:, None, :]
    scores = jnp.einsum("bpd,dh->bhp", patches, probe, preferred_element_type=jnp.float32)
    scores = jnp.where(live, scores, -1e30)
    peak = jnp.max(scores, axis=2, keepdims=True)
    raised = jnp.where(live, jnp.exp(scores - peak), 0.0)
    attend = raised / jnp.sum(raised, axis=2, keepdims=True)
    moments16 = jnp.einsum(
        "bhp,bpd->bhd", attend.astype(jnp.bfloat16), patches, preferred_element_type=jnp.float32
    ).astype(jnp.bfloat16)
    pooled16 = (
        jnp.einsum("bhd,dhe->bhe", moments16, w_value, preferred_element_type=jnp.float32)
        .reshape(images, local_width)
        .astype(jnp.bfloat16)
    )
    partial_value = jnp.dot(pooled16, out_weight, preferred_element_type=jnp.float32)

    along_x = lax.psum(partial_value, "mp", axis_index_groups=X_GROUPS)
    along_x, text_all = lax.optimization_barrier((along_x, text_all))
    mp = lax.axis_size("mp")
    embedding = along_x + lax.ppermute(
        along_x, "mp", [(i, (i + mp // 2) % mp) for i in range(mp)]
    )

    text_rows = text_all.reshape(total, width)
    text_f = text_rows.astype(jnp.float32)
    text_norm = jnp.sqrt(jnp.sum(text_f * text_f, axis=1) + 1e-06)
    text_unit = text_f / text_norm[:, None]

    norm = jnp.sqrt(jnp.sum(embedding * embedding, axis=1, keepdims=True) + 1e-06)
    unit = embedding / norm
    cosine = jnp.dot(unit, text_unit.T, precision=HIGHEST)
    columns = jnp.arange(total, dtype=jnp.int32)
    sign = jnp.where(pos_text[:, None] == columns[None, :], 1.0, -1.0)
    slope = -sign * jax.nn.sigmoid(-sign * (temper * cosine + offset))
    grad = temper * jnp.dot(slope, text_unit, precision=HIGHEST)
    grad_embed = (grad - unit * jnp.sum(unit * grad, axis=1, keepdims=True)) / norm
    grad_pooled = jnp.dot(grad_embed, out_weight.astype(jnp.float32).T, precision=HIGHEST)
    grad_heads = grad_pooled.reshape(images, heads, HEAD_DIM)
    grad_moments = jnp.einsum(
        "bhe,dhe->bhd", grad_heads, w_value.astype(jnp.float32), precision=HIGHEST
    ).astype(jnp.bfloat16)
    grad_attend = jnp.einsum(
        "bpd,bhd->bhp", patches, grad_moments, preferred_element_type=jnp.float32
    )
    grad_scores = attend * (grad_attend - jnp.sum(attend * grad_attend, axis=2, keepdims=True))
    key_moments = jnp.einsum(
        "bhp,bpd->hd",
        grad_scores.astype(jnp.bfloat16),
        patches,
        preferred_element_type=jnp.float32,
    )

    part = width // XS
    half = part // 2
    core = lax.axis_index("dp") % 2
    x_at = lax.axis_index("mp") % XS * part
    unit_own = lax.dynamic_slice_in_dim(unit, x_at + core * half, half, axis=1)
    unit_other = lax.dynamic_slice_in_dim(unit, x_at + (1 - core) * half, half, axis=1)
    swapped = lax.ppermute(
        jnp.concatenate([slope, unit_other], axis=1), "dp", [(i, i ^ 1) for i in range(dp)]
    )
    key_moments, swapped = lax.optimization_barrier((key_moments, swapped))

    slopes = jnp.concatenate([slope, swapped[:, :total]], axis=0)
    units = jnp.concatenate([unit_own, swapped[:, total:]], axis=0)
    for_texts = temper * lax.dot_general(
        slopes, units, (((0,), (0,)), ((), ())), precision=HIGHEST
    ).reshape(dp, images, half)
    text_high, text_low = halves(for_texts)
    grad_high, grad_low = halves(grad_pooled)
    factors = jnp.concatenate([grad_high, grad_low, pooled16.astype(jnp.float32)], axis=1)
    sliced = jnp.concatenate([grad_embed[:, None], key_moments[:, None]], axis=1)
    sliced = jnp.concatenate([moments16.astype(jnp.float32), *halves(sliced)], axis=1)
    sliced = lax.optimization_barrier(sliced)
    kinds = sliced.shape[1]
    sliced = (
        sliced.reshape(images, kinds, dp, rows)
        .transpose(2, 0, 1, 3)
        .reshape(dp, images, kinds * rows)
    )
    factor_at = 2 * half
    slice_at = factor_at + 3 * local_width
    used = slice_at + kinds * rows
    size = used + -used % 128

    def place(values, at):
        return jnp.pad(values, ((0, 0), (0, 0), (at, size - at - values.shape[2])))

    sent = (
        place(text_high, 0)
        + place(text_low, half)
        + place(factors[None], factor_at)
        + place(sliced, slice_at)
    ).astype(jnp.bfloat16)
    got = lax.all_to_all(sent, "dp", 0, 0, tiled=True)

    text_sums = jnp.sum(
        got[:, :, :factor_at].astype(jnp.float32).reshape(dp // 2, 2, images, factor_at), axis=0
    )
    text_part = (text_sums[..., :half] + text_sums[..., half:]).transpose(1, 0, 2)
    text_part = text_part.reshape(images, part)
    text_part, got = lax.optimization_barrier((text_part, got))
    text_parts = spread(text_part, X_GROUPS, "mp", XS)
    got_rows = got[:, :, factor_at:used].astype(jnp.float32).reshape(total, used - factor_at)
    at = 3 * local_width
    grads_all = whole(got_rows[:, : 2 * local_width]).reshape(total, heads, HEAD_DIM)
    pooled_all = got_rows[:, 2 * local_width : at]
    sliced_all = got_rows[:, at:].reshape(total, kinds, rows)
    moments_all = sliced_all[:, :heads]
    columns_all = sliced_all[:, heads] + sliced_all[:, heads + 2]
    key_sum = jnp.sum(
        (sliced_all[:, heads + 1] + sliced_all[:, heads + 3]).reshape(dp, images, rows), axis=0
    )
    value_grad = jnp.einsum("bhd,bhe->dhe", moments_all, grads_all, precision=HIGHEST).reshape(
        rows, local_width
    )
    out_grad = jnp.dot(pooled_all.T, columns_all, precision=HIGHEST)
    key_grad = (key_sum.T[:, :, None] * q_heads[None] / head_root).reshape(rows, local_width)
    kv_grad = jnp.stack([key_grad, value_grad], axis=1)

    grad_txt = text_parts.transpose(1, 0, 2).reshape(images, width)
    own_text = texts.astype(jnp.float32)
    own_norm = jnp.sqrt(jnp.sum(own_text * own_text, axis=1, keepdims=True) + 1e-06)
    own_unit = own_text / own_norm
    text_grad = (
        grad_txt - own_unit * jnp.sum(own_unit * grad_txt, axis=1, keepdims=True)
    ) / own_norm
    return (kv_grad, out_grad, text_grad)


def solution(mesh):
    in_specs = (
        P("dp", None, None),
        P("dp"),
        P("dp"),
        P("dp", None),
        P(None, None, "mp"),
        P("mp", None),
        P("mp"),
        P(),
        P(),
    )
    out_specs = (P("dp", None, "mp"), P("mp", "dp"), P("dp", None))
    return jax.shard_map(local, mesh=mesh, in_specs=in_specs, out_specs=out_specs, check_vma=False)
```
